256 devices in a mesh: tm: 16 (over y, x_hi, core), space: 16 (over z, x_lo).
Axes of the slice: x: 4 (x_hi: 2, x_lo: 2; x = x_hi * 2 + x_lo), y: 4, z: 8, core: 2. Of those that a mesh axis runs over, the one named last changes fastest.
Arguments:
- current: bfloat16 [32, 64, 256, 128], P('tm', None, 'space'), may hold values from -6 to 6
- contexts: bfloat16 [32, 64, 256, 128], P('tm', None, 'space'), may hold values from -6 to 6
- cotangent: bfloat16 [32, 64, 256, 128], P('tm', None, 'space'), may hold values from -6 to 6
- level_table: int32 [32], P('tm'), may hold values from 1 to 2, as said below
- ref_table: int32 [32, 2], P('tm'), may hold values from -1 to 32, as said below
- w_first: bfloat16 [2, 9, 64, 192], replicated, may hold values from -0.25 to 0.25
- w_rest: bfloat16 [2, 4, 9, 64, 64], replicated, may hold values from -0.375 to 0.375
Outputs:
- output: bfloat16 [32, 64, 256, 128], P('tm', None, 'space')
- ref_grad: float32 [32, 64, 256, 128], P('tm', None, 'space')
The draws below stay inside these ranges and needn't reach their ends.
Inputs may be any that keep to these rules, and one draw needn't show every extreme that they name: level_table[f] is 1 for the frames f with (f + p) % 4 == 0 and 2 for the others, p one drawn phase of 0 to 3. ref_table[f, 0] = f - d and ref_table[f, 1] = f + d with d = 4 for level 1 and d = 2 for level 2, without wrapping; a reference before the window is stored as -1 and one after it as 32.
All inputs are finite; a program needn't handle non-finite values.
Results may differ from the reference program's by a relative error of at most 0.02.
Values may be sent and summed in bfloat16 or wider, within the bound.
A program may use at most 64 MiB of HBM per device.

```python
import jax
import jax.numpy as jnp
from jax import lax

CH = 64
COLS = 128
LAYERS = 5
FRAMES = 32
HEIGHT = 256


def level_rule(key):
    phase = jax.random.randint(key, (), 0, 4).astype(jnp.int32)
    frame_ids = jnp.arange(FRAMES, dtype=jnp.int32)
    levels = jnp.where((frame_ids + phase) % 4 == 0, 1, 2).astype(jnp.int32)
    return (frame_ids, levels)


def draw_level_table(key, part):
    frame_ids, levels = level_rule(key)
    return levels


def draw_ref_table(key, part):
    frame_ids, levels = level_rule(key)
    distance = 2 * (3 - levels)
    table = jnp.stack([frame_ids - distance, frame_ids + distance], 1)
    return jnp.clip(table, -1, FRAMES).astype(jnp.int32)


def steps_of(key, extent, split, smallest, top_value):
    gain, own = 1.0, jax.random.fold_in(key, 6)
    for axis_at, blocks in split:
        draws = jnp.exp(jax.random.uniform(jax.random.fold_in(own, axis_at), (blocks,), jnp.float32, smallest / len(split), top_value / len(split)))
        gain = gain * jnp.repeat(draws, extent[axis_at] // blocks).reshape([-1 if axis == axis_at else 1 for axis in range(len(extent))])
    return gain


def scatter_about(rng, extent, scale, limit, pieces=(), kind=jnp.bfloat16):
    result = jax.random.normal(rng, extent, jnp.float32) * scale
    if len(pieces) > 0:
        result = steps_of(rng, extent, pieces, -0.22, 0.18) * result
    return jnp.clip(result, min=-limit, max=limit).astype(kind)


def setup_inputs(seed: int = 0) -> dict:
    streams_of = jax.random.split(jax.random.key(seed), 8)
    return {
        "current": scatter_about(streams_of[0], (FRAMES, CH, HEIGHT, COLS), 1.0, 6.0, ((0, 16), (2, 16))),
        "contexts": scatter_about(streams_of[1], (FRAMES, CH, HEIGHT, COLS), 1.0, 6.0, ((0, 16), (2, 16))),
        "cotangent": scatter_about(streams_of[2], (FRAMES, CH, HEIGHT, COLS), 1.0, 6.0, ((0, 16), (2, 16))),
        "level_table": draw_level_table(jax.random.fold_in(streams_of[7], 71), 0),
        "ref_table": draw_ref_table(jax.random.fold_in(streams_of[7], 71), 0),
        "w_first": scatter_about(streams_of[5], (2, 9, CH, 3 * CH), (9 * CH) ** -0.5, 0.25),
        "w_rest": scatter_about(streams_of[6], (2, LAYERS - 1, 9, CH, CH), (9 * CH // 2) ** -0.5, 0.375),
    }


def conv_frame(padded, weights):
    row_count = padded.shape[1] - 2
    col_count = padded.shape[2]
    widened = jnp.pad(padded, ((0, 0), (0, 0), (1, 1))).astype(jnp.float32)
    tap_weights = weights.astype(jnp.float32)
    summed = jnp.zeros((tap_weights.shape[1], row_count, col_count), jnp.float32)
    for tap_index in range(9):
        row_shift = tap_index // 3
        col_shift = tap_index % 3
        window = widened[:, row_shift:row_shift + row_count, col_shift:col_shift + col_count]
        summed = summed + jnp.einsum("oc,chw->ohw", tap_weights[tap_index], window)
    return summed


def add_rims(field):
    return jnp.pad(field, ((0, 0), (1, 1), (0, 0)))


def flipped(weights):
    return jnp.swapaxes(jnp.flip(weights, 0), 1, 2)


def silu_slope(preact):
    sigma = jax.nn.sigmoid(preact)
    return sigma * (1.0 + preact * (1.0 - sigma))


def reference(current, contexts, cotangent, level_table, ref_table, w_first, w_rest):
    channels = contexts.shape[1]
    frame_total = contexts.shape[0]
    mid_count = w_rest.shape[1] - 1
    inside = (ref_table >= 0) & (ref_table < frame_total)
    clipped = jnp.clip(ref_table, 0, frame_total - 1).astype(jnp.int32)

    def fetch(frame_index, side):
        return jnp.where(inside[frame_index, side], contexts[clipped[frame_index, side]], jnp.zeros_like(contexts[0]))

    def one_frame(frame_index):
        level_one = level_table[frame_index] == 1
        first_taps = jnp.where(level_one, w_first[0], w_first[1])
        rest_taps = jnp.where(level_one, w_rest[0], w_rest[1])
        joined = jnp.concatenate([current[frame_index], fetch(frame_index, 0), fetch(frame_index, 1)], 0)
        preacts = []
        preact = conv_frame(add_rims(joined), first_taps)
        preacts.append(preact)
        activation = jax.nn.silu(preact).astype(jnp.bfloat16)
        for layer_index in range(mid_count):
            preact = conv_frame(add_rims(activation), rest_taps[layer_index])
            preacts.append(preact)
            activation = jax.nn.silu(preact).astype(jnp.bfloat16)
        final_term = conv_frame(add_rims(activation), rest_taps[mid_count])
        output = (current[frame_index].astype(jnp.float32) + final_term).astype(jnp.bfloat16)
        gradient = conv_frame(add_rims(cotangent[frame_index]), flipped(rest_taps[mid_count]))
        for layer_index in reversed(range(mid_count)):
            slope = (gradient * silu_slope(preacts[layer_index + 1])).astype(jnp.bfloat16)
            gradient = conv_frame(add_rims(slope), flipped(rest_taps[layer_index]))
        slope = (gradient * silu_slope(preacts[0])).astype(jnp.bfloat16)
        context_grad = conv_frame(add_rims(slope), flipped(first_taps[:, :, channels:]))
        behind_grad = context_grad[:channels].astype(jnp.bfloat16)
        forward_grad = context_grad[channels:].astype(jnp.bfloat16)
        return output, behind_grad, forward_grad

    output, behind_grad, forward_grad = lax.map(one_frame, jnp.arange(current.shape[0], dtype=jnp.int32))
    keep_behind = inside[:, 0][:, None, None, None]
    keep_forward = inside[:, 1][:, None, None, None]
    ref_grad = jnp.zeros(current.shape, jnp.float32)
    ref_grad = ref_grad.at[clipped[:, 0]].add(jnp.where(keep_behind, behind_grad.astype(jnp.float32), 0.0))
    ref_grad = ref_grad.at[clipped[:, 1]].add(jnp.where(keep_forward, forward_grad.astype(jnp.float32), 0.0))
    return output, ref_grad
```

```python
import jax
import jax.numpy as jnp
from jax import lax
from jax.experimental import pallas as pl
from jax.experimental.pallas import tpu as pltpu
from jax.sharding import PartitionSpec as P

MESH = pl.DeviceIdType.MESH
F32 = jnp.float32
BF = jnp.bfloat16
C = 64
W = 128
H = 16
ODD, EVEN = 0, 1


def lanes(start, count):
    return slice(start * W, (start + count) * W)


def shifted(a):
    n = a.shape[1]
    lane = lax.broadcasted_iota(jnp.int32, a.shape, 1) & (W - 1)
    left = jnp.where(lane == 0, 0.0, pltpu.roll(a, 1, 1))
    right = jnp.where(lane == W - 1, 0.0, pltpu.roll(a, n - 1, 1))
    return left, right


def put(ref, where, a, flip=False, base=0):
    left, right = shifted(a)
    first, last = (right, left) if flip else (left, right)
    ref[base : base + C, where] = first.astype(BF)
    ref[base + C : base + 2 * C, where] = a.astype(BF)
    ref[base + 2 * C : base + 3 * C, where] = last.astype(BF)


def conv(weights, stack, flip=False, out_channels=C):
    t = jnp.dot(weights, stack, preferred_element_type=F32)
    rows = stack.shape[1] // W - 2
    o = out_channels
    first, last = (t[2 * o : 3 * o], t[0:o]) if flip else (t[0:o], t[2 * o : 3 * o])
    return first[:, lanes(0, rows)] + t[o : 2 * o, lanes(1, rows)] + last[:, lanes(2, rows)]


def body(
    nt, ns, level, cur, ctx, cot, wf, wr, out, rg,
    flat, tctx, flag_s, flag_r, mctx, sel_o, sel_l, x_o, x_l, m_l, tcur, tcot,
    stack, stack_c, stack_g, stack_3, p1_cur, g4, p1, d1, d2, d3, d4, outs,
    h1_s, h1_r, h3_s, h3_r, om_s, om_r, ox_s, ox_r, em_s, em_r, ex_s, ex_r, ey_r,
    w_fwd, w_bwd, w_ctx, w_back, ssem, rsem,
):
    tm = lax.axis_index("tm")
    sp = lax.axis_index("space")
    core = lax.rem(tm, 2)
    mate = tm + 1 - 2 * core
    cross = tm - 1 + 2 * core
    cross_ok = (cross >= 0) & (cross < nt)
    up_ok = sp < ns - 1
    dn_ok = sp > 0
    always = tm >= 0
    sent = []

    def link(i, src, dst, device):
        return pltpu.make_async_remote_copy(
            src_ref=src, dst_ref=dst, send_sem=ssem.at[i], recv_sem=rsem.at[i],
            device_id=device, device_id_type=MESH,
        )

    def send(i, src, dst, device, ok):
        @pl.when(ok)
        def _():
            link(i, src, dst, device).start()

        sent.append((i, src, dst, device, ok))

    def arrive(i, src, dst, ok):
        @pl.when(ok)
        def _():
            link(i, src, dst, (tm, sp)).wait_recv()

    partners = []
    for who, who_ok in ((mate, always), (cross, cross_ok)):
        partners.append((who, sp, who_ok))
        partners.append((who, sp + 1, who_ok & up_ok))
        partners.append((who, sp - 1, who_ok & dn_ok))
    partners.append((tm, sp + 1, up_ok))
    partners.append((tm, sp - 1, dn_ok))
    barrier = pltpu.get_barrier_semaphore()
    for a, b, ok in partners:
        @pl.when(ok)
        def _():
            pl.semaphore_signal(barrier, inc=1, device_id=(a, b), device_id_type=MESH)

    def rows_first(src, i, dst, row0):
        flat[...] = src[i].astype(F32).reshape(C * H, W)
        for r in range(H):
            dst[i, :, lanes(row0 + r, 1)] = flat[pl.ds(r, C, stride=H), :].astype(BF)

    has_l0 = level[0] == 1
    has_l1 = level[1] == 1
    has_l = has_l0 | has_l1
    flag_s[...] = jnp.full((16, W), jnp.where(has_l0, 1.0, 0.0), F32).astype(BF)
    for i in range(2):
        rows_first(ctx, i, tctx, 0)
    spans = 1 + up_ok.astype(jnp.int32) + dn_ok.astype(jnp.int32)
    pl.semaphore_wait(barrier, spans * (2 + cross_ok.astype(jnp.int32)) - 1)

    send(0, flag_s, flag_r, (mate, sp), always)
    send(1, tctx, mctx.at[:, :, lanes(1, H)], (mate, sp), always)
    send(2, tctx.at[:, :, lanes(H - 1, 1)], mctx.at[:, :, lanes(0, 1)], (mate, sp + 1), up_ok)
    send(3, tctx.at[:, :, lanes(0, 1)], mctx.at[:, :, lanes(H + 1, 1)], (mate, sp - 1), dn_ok)
    for i in range(2):
        rows_first(cur, i, tcur, 1)
    send(4, tcur.at[:, :, lanes(H, 1)], tcur.at[:, :, lanes(0, 1)], (tm, sp + 1), up_ok)
    send(5, tcur.at[:, :, lanes(1, 1)], tcur.at[:, :, lanes(H + 1, 1)], (tm, sp - 1), dn_ok)

    arrive(0, flag_s, flag_r, always)
    mate_l0 = jnp.broadcast_to(flag_r[0:1, :].astype(F32), (C, W))
    even0 = jnp.maximum(mate_l0, jnp.where(has_l0, 1.0, 0.0))
    even_first = even0 > 0.5

    def wide(n):
        return jnp.concatenate([even0] * n, axis=1) > 0.5

    def pick(which, zero, one):
        zero, one = zero.astype(F32), one.astype(F32)
        mask = wide(zero.shape[1] // W)
        return jnp.where(mask, zero, one) if which == EVEN else jnp.where(mask, one, zero)

    sel_o[...] = pick(ODD, tctx[0], tctx[1]).astype(BF)
    send(6, sel_o, x_o.at[:, lanes(1, H)], (cross, sp), cross_ok)
    send(7, sel_o.at[:, lanes(H - 1, 1)], x_o.at[:, lanes(0, 1)], (cross, sp + 1), cross_ok & up_ok)
    send(8, sel_o.at[:, lanes(0, 1)], x_o.at[:, lanes(H + 1, 1)], (cross, sp - 1), cross_ok & dn_ok)
    arrive(1, tctx, mctx.at[:, :, lanes(1, H)], always)
    mate_even = pick(EVEN, mctx[0, :, lanes(1, H)], mctx[1, :, lanes(1, H)])
    sel_l[...] = jnp.where(has_l, pick(EVEN, tctx[0], tctx[1]), mate_even).astype(BF)
    send(9, sel_l, x_l.at[:, lanes(1, H)], (cross, sp), cross_ok)
    send(10, sel_l.at[:, lanes(H - 1, 1)], x_l.at[:, lanes(0, 1)], (cross, sp + 1), cross_ok & up_ok)
    send(11, sel_l.at[:, lanes(0, 1)], x_l.at[:, lanes(H + 1, 1)], (cross, sp - 1), cross_ok & dn_ok)

    for i in range(2):
        rows_first(cot, i, tcot, 2)
    send(12, tcot.at[:, :, lanes(H, 2)], tcot.at[:, :, lanes(0, 2)], (tm, sp + 1), up_ok)
    send(13, tcot.at[:, :, lanes(2, 2)], tcot.at[:, :, lanes(H + 2, 2)], (tm, sp - 1), dn_ok)

    def clear(ok, ref, where, lead):
        @pl.when(jnp.logical_not(ok))
        def _():
            for c in range(lead):
                view = ref.at[c] if lead > 1 else ref
                n = where.stop - where.start
                view[:, where] = jnp.zeros((C, n), BF)

    clear(dn_ok, tcur, lanes(0, 1), 2)
    clear(up_ok, tcur, lanes(H + 1, 1), 2)
    clear(dn_ok, tcot, lanes(0, 2), 2)
    clear(up_ok, tcot, lanes(H + 2, 2), 2)
    clear(dn_ok, mctx, lanes(0, 1), 2)
    clear(up_ok, mctx, lanes(H + 1, 1), 2)
    for ref in (x_o, x_l):
        clear(cross_ok, ref, lanes(1, H), 1)
        clear(cross_ok & dn_ok, ref, lanes(0, 1), 1)
        clear(cross_ok & up_ok, ref, lanes(H + 1, 1), 1)
    mate_cross = tm + 2 - 4 * core
    mate_cross_ok = (mate_cross >= 0) & (mate_cross < nt)
    clear(mate_cross_ok, m_l, lanes(0, H + 2), 1)
    for c in range(2):
        clear(dn_ok, h1_r.at[c, 0], lanes(0, 4), 1)
        clear(up_ok, h1_r.at[c, 1], lanes(0, 4), 1)
        clear(dn_ok, h3_r.at[c, 0], lanes(0, 3), 1)
        clear(up_ok, h3_r.at[c, 1], lanes(0, 3), 1)
    clear(cross_ok, ox_r, lanes(0, H), 1)
    clear(cross_ok, ex_r, lanes(0, H), 1)
    clear(mate_cross_ok, ey_r, lanes(0, H), 1)

    eye_r = lax.broadcasted_iota(jnp.int32, (3 * C, 3 * C), 0)
    eye_c = lax.broadcasted_iota(jnp.int32, (3 * C, 3 * C), 1)
    eye = jnp.where(eye_r == eye_c, 1.0, 0.0).astype(BF)

    def turned(m):
        return lax.dot_general(
            eye[: m.shape[1], : m.shape[1]], m, (((1,), (1,)), ((), ())), preferred_element_type=F32
        ).astype(BF)

    for c in (ODD, EVEN):
        def first_tap(t):
            if c == ODD:
                return wf[1, t]
            return jnp.where(has_l, wf[0, t].astype(F32), wf[1, t].astype(F32)).astype(BF)

        def rest_tap(k, t):
            if c == ODD:
                return wr[1, k, t]
            return jnp.where(has_l, wr[0, k, t].astype(F32), wr[1, k, t].astype(F32)).astype(BF)

        taps = [first_tap(t) for t in range(9)]
        for g in range(3):
            part = [tap[:, g * C : (g + 1) * C] for tap in taps]
            for a in range(3):
                rows = jnp.concatenate(part[3 * a : 3 * a + 3], axis=1)
                if g == 0:
                    w_fwd[c, 0, a * C : (a + 1) * C, :] = rows
                else:
                    w_ctx[c, a * C : (a + 1) * C, (g - 1) * 3 * C : g * 3 * C] = rows
        both = [tap[:, C:] for tap in taps]
        for a in range(3):
            m = jnp.concatenate([both[3 * a + b] for b in range(3)], axis=0)
            w_back[c, a * 2 * C : (a + 1) * 2 * C, :] = turned(m)
        for k in range(4):
            part = [rest_tap(k, t) for t in range(9)]
            for a in range(3):
                w_fwd[c, k + 1, a * C : (a + 1) * C, :] = jnp.concatenate(part[3 * a : 3 * a + 3], axis=1)
                m = jnp.concatenate([part[3 * a + b] for b in range(3)], axis=0)
                w_bwd[c, k, a * C : (a + 1) * C, :] = turned(m)

    arrive(4, tcur.at[:, :, lanes(H, 1)], tcur.at[:, :, lanes(0, 1)], dn_ok)
    arrive(5, tcur.at[:, :, lanes(1, 1)], tcur.at[:, :, lanes(H + 1, 1)], up_ok)
    for c in (ODD, EVEN):
        put(stack, lanes(0, H + 2), pick(c, tcur[0], tcur[1]))
        p1_cur[c] = conv(w_fwd[c, 0], stack[:, lanes(0, H + 2)])
    arrive(12, tcot.at[:, :, lanes(H, 2)], tcot.at[:, :, lanes(0, 2)], dn_ok)
    arrive(13, tcot.at[:, :, lanes(2, 2)], tcot.at[:, :, lanes(H + 2, 2)], up_ok)
    for c in (ODD, EVEN):
        put(stack_g, lanes(0, H + 4), pick(c, tcot[0], tcot[1]), flip=True)
        g4[c] = conv(w_bwd[c, 3], stack_g[:, lanes(0, H + 4)], flip=True)

    arrive(2, tctx.at[:, :, lanes(H - 1, 1)], mctx.at[:, :, lanes(0, 1)], dn_ok)
    arrive(3, tctx.at[:, :, lanes(0, 1)], mctx.at[:, :, lanes(H + 1, 1)], up_ok)
    first_core = core == 0

    def layer_one(c, outer, inner):
        put(stack_c, lanes(0, H + 2), jnp.where(first_core, outer, inner))
        put(stack_c, lanes(0, H + 2), jnp.where(first_core, inner, outer), base=3 * C)
        pre = p1_cur[c] + conv(w_ctx[c], stack_c[...])
        p1[c, :, lanes(4, H)] = pre
        h1_s[c, 0] = pre[:, lanes(H - 4, 4)].astype(BF)
        h1_s[c, 1] = pre[:, lanes(0, 4)].astype(BF)
        send(14 + 2 * c, h1_s.at[c, 0], h1_r.at[c, 0], (tm, sp + 1), up_ok)
        send(15 + 2 * c, h1_s.at[c, 1], h1_r.at[c, 1], (tm, sp - 1), dn_ok)

    def activate(pre, halo):
        sigma = 1.0 / (1.0 + jnp.exp(-pre))
        act = pre * sigma
        slope = sigma * (1.0 + pre * (1.0 - sigma))
        row = (lax.broadcasted_iota(jnp.int32, pre.shape, 1) >> 7) + (sp * H - halo)
        inside = (row >= 0) & (row < ns * H)
        return jnp.where(inside, act, 0.0), jnp.where(inside, slope, 0.0)

    def forward(c):
        arrive(14 + 2 * c, h1_s.at[c, 0], h1_r.at[c, 0], dn_ok)
        arrive(15 + 2 * c, h1_s.at[c, 1], h1_r.at[c, 1], up_ok)
        p1[c, :, lanes(0, 4)] = h1_r[c, 0].astype(F32)
        p1[c, :, lanes(H + 4, 4)] = h1_r[c, 1].astype(F32)
        act, slope = activate(p1[c], 4)
        d1[c] = slope[:, lanes(3, H + 2)]
        put(stack, lanes(0, 24), act)
        act, slope = activate(conv(w_fwd[c, 1], stack[...]), 3)
        d2[c] = slope[:, lanes(1, H + 4)]
        put(stack, lanes(0, 22), act)
        act, slope = activate(conv(w_fwd[c, 2], stack[:, lanes(0, 22)]), 2)
        d3[c] = slope[:, lanes(2, H)]
        put(stack, lanes(0, 20), act)
        act, slope = activate(conv(w_fwd[c, 3], stack[:, lanes(0, 20)]), 1)
        put(stack_g, lanes(0, 18), g4[c] * slope, flip=True)
        s3 = conv(w_bwd[c, 2], stack_g[:, lanes(0, 18)], flip=True) * d3[c]
        h3_s[c, 0] = s3[:, lanes(H - 3, 3)].astype(BF)
        h3_s[c, 1] = s3[:, lanes(0, 3)].astype(BF)
        send(18 + 2 * c, h3_s.at[c, 0], h3_r.at[c, 0], (tm, sp + 1), up_ok)
        send(19 + 2 * c, h3_s.at[c, 1], h3_r.at[c, 1], (tm, sp - 1), dn_ok)
        put(stack_3.at[c], lanes(3, H), s3, flip=True)
        put(stack, lanes(0, 18), act)
        own = pick(c, tcur[0, :, lanes(1, H)], tcur[1, :, lanes(1, H)])
        outs[c] = own + conv(w_fwd[c, 4], stack[:, lanes(0, 18)])

    def backward(c):
        arrive(18 + 2 * c, h3_s.at[c, 0], h3_r.at[c, 0], dn_ok)
        arrive(19 + 2 * c, h3_s.at[c, 1], h3_r.at[c, 1], up_ok)
        put(stack_3.at[c], lanes(0, 3), h3_r[c, 0].astype(F32), flip=True)
        put(stack_3.at[c], lanes(H + 3, 3), h3_r[c, 1].astype(F32), flip=True)
        s2 = conv(w_bwd[c, 1], stack_3[c], flip=True) * d2[c]
        put(stack_g, lanes(0, 20), s2, flip=True)
        s1 = conv(w_bwd[c, 0], stack_g[:, lanes(0, 20)], flip=True) * d1[c]
        put(stack_g, lanes(0, 18), s1, flip=True)
        grads = conv(w_back[c], stack_g[:, lanes(0, 18)], flip=True, out_channels=2 * C)
        behind, ahead = grads[:C], grads[C:]
        return jnp.where(first_core, behind, ahead), jnp.where(first_core, ahead, behind)

    arrive(6, sel_o, x_o.at[:, lanes(1, H)], cross_ok)
    arrive(7, sel_o.at[:, lanes(H - 1, 1)], x_o.at[:, lanes(0, 1)], cross_ok & dn_ok)
    arrive(8, sel_o.at[:, lanes(0, 1)], x_o.at[:, lanes(H + 1, 1)], cross_ok & up_ok)
    layer_one(ODD, x_o[...].astype(F32), pick(ODD, mctx[0], mctx[1]))
    arrive(9, sel_l, x_l.at[:, lanes(1, H)], cross_ok)
    arrive(10, sel_l.at[:, lanes(H - 1, 1)], x_l.at[:, lanes(0, 1)], cross_ok & dn_ok)
    arrive(11, sel_l.at[:, lanes(0, 1)], x_l.at[:, lanes(H + 1, 1)], cross_ok & up_ok)
    send(22, x_l, m_l, (mate, sp), cross_ok)
    forward(ODD)
    arrive(22, x_l, m_l, mate_cross_ok)
    inner = jnp.where(has_l, m_l[...].astype(F32), pick(EVEN, mctx[0], mctx[1]))
    layer_one(EVEN, x_l[...].astype(F32), inner)
    outer_g, inner_g = backward(ODD)
    ox_s[...] = outer_g.astype(BF)
    send(23, ox_s, ox_r, (cross, sp), cross_ok)
    om_s[...] = inner_g.astype(BF)
    send(24, om_s, om_r, (mate, sp), always)
    forward(EVEN)
    outer_g, inner_g = backward(EVEN)
    em_s[...] = inner_g.astype(BF)
    send(25, em_s, em_r, (mate, sp), always)
    arrive(25, em_s, em_r, always)
    from_mate = em_r[...].astype(F32)
    ex_s[...] = (outer_g + jnp.where(has_l, 0.0, from_mate)).astype(BF)
    send(26, ex_s, ex_r, (cross, sp), cross_ok)
    mask = wide(H)
    out[0] = jnp.where(mask, outs[EVEN], outs[ODD]).astype(BF)
    out[1] = jnp.where(mask, outs[ODD], outs[EVEN]).astype(BF)
    arrive(23, ox_s, ox_r, cross_ok)
    arrive(24, om_s, om_r, always)
    odd_g = ox_r[...].astype(F32) + om_r[...].astype(F32)
    arrive(26, ex_s, ex_r, cross_ok)
    send(27, ex_r, ey_r, (mate, sp), cross_ok)
    arrive(27, ex_r, ey_r, mate_cross_ok)
    even_g = ex_r[...].astype(F32) + ey_r[...].astype(F32) + from_mate
    even_g = jnp.where(has_l, even_g, 0.0)
    rg[0] = jnp.where(mask, even_g, odd_g)
    rg[1] = jnp.where(mask, odd_g, even_g)
    for i, src, dst, device, ok in sent:
        @pl.when(ok)
        def _():
            link(i, src, dst, device).wait_send()


def solution(mesh):
    nt, ns = mesh.shape["tm"], mesh.shape["space"]

    def on_device(current, contexts, cotangent, level_table, ref_table, w_first, w_rest):
        vmem = pl.BlockSpec(memory_space=pltpu.VMEM)

        def bf(*shape):
            return pltpu.VMEM(shape, BF)

        def f32(*shape):
            return pltpu.VMEM(shape, F32)

        slab = H * W
        halo = (H + 2) * W
        scratch = [
            f32(C * H, W), bf(2, C, slab), bf(16, W), bf(16, W), bf(2, C, halo), bf(C, slab), bf(C, slab),
            bf(C, halo), bf(C, halo), bf(C, halo), bf(2, C, halo), bf(2, C, (H + 4) * W),
            bf(3 * C, 24 * W), bf(6 * C, halo), bf(3 * C, 20 * W), bf(2, 3 * C, 22 * W),
            f32(2, C, slab), f32(2, C, halo), f32(2, C, 24 * W),
            f32(2, C, halo), f32(2, C, (H + 4) * W), f32(2, C, slab), f32(2, C, halo), f32(2, C, slab),
            bf(2, 2, C, 4 * W), bf(2, 2, C, 4 * W), bf(2, 2, C, 3 * W), bf(2, 2, C, 3 * W),
            bf(C, slab), bf(C, slab), bf(C, slab), bf(C, slab),
            bf(C, slab), bf(C, slab), bf(C, slab), bf(C, slab), bf(C, slab),
            bf(2, 5, 3 * C, 3 * C), bf(2, 4, 3 * C, 3 * C), bf(2, 3 * C, 6 * C), bf(2, 6 * C, 3 * C),
            pltpu.SemaphoreType.DMA((28,)), pltpu.SemaphoreType.DMA((28,)),
        ]

        def kernel(*refs):
            body(nt, ns, *refs)

        out, rg = pl.pallas_call(
            kernel,
            out_shape=(
                jax.ShapeDtypeStruct((2, C, slab), BF),
                jax.ShapeDtypeStruct((2, C, slab), F32),
            ),
            in_specs=[pl.BlockSpec(memory_space=pltpu.SMEM)] + [vmem] * 5,
            out_specs=(vmem, vmem),
            scratch_shapes=scratch,
            compiler_params=pltpu.CompilerParams(
                collective_id=0, has_side_effects=True, vmem_limit_bytes=56 << 20
            ),
            name="coding",
        )(level_table, current, contexts, cotangent, w_first, w_rest)
        return out.reshape(2, C, H, W), rg.reshape(2, C, H, W)

    frames = P("tm", None, "space", None)
    return jax.shard_map(
        on_device,
        mesh=mesh,
        in_specs=(frames, frames, frames, P("tm"), P("tm", None), P(), P()),
        out_specs=(frames, frames),
        check_vma=False,
    )
```

```python
import jax
import jax.numpy as jnp
from jax import lax
from jax.experimental import pallas as pl
from jax.experimental.pallas import tpu as pltpu
from jax.sharding import PartitionSpec as P

MESH = pl.DeviceIdType.MESH
F32 = jnp.float32
BF = jnp.bfloat16
C = 64
W = 128
H = 16
ODD, EVEN = 0, 1


def lanes(start, count):
    return slice(start * W, (start + count) * W)


def shifted(a):
    n = a.shape[1]
    lane = lax.broadcasted_iota(jnp.int32, a.shape, 1) & (W - 1)
    left = jnp.where(lane == 0, 0.0, pltpu.roll(a, 1, 1))
    right = jnp.where(lane == W - 1, 0.0, pltpu.roll(a, n - 1, 1))
    return left, right


def put(ref, where, a, flip=False, base=0):
    left, right = shifted(a)
    first, last = (right, left) if flip else (left, right)
    ref[base : base + C, where] = first.astype(BF)
    ref[base + C : base + 2 * C, where] = a.astype(BF)
    ref[base + 2 * C : base + 3 * C, where] = last.astype(BF)


def conv(weights, stack, flip=False, out_channels=C):
    t = jnp.dot(weights, stack, preferred_element_type=F32)
    rows = stack.shape[1] // W - 2
    o = out_channels
    first, last = (t[2 * o : 3 * o], t[0:o]) if flip else (t[0:o], t[2 * o : 3 * o])
    return first[:, lanes(0, rows)] + t[o : 2 * o, lanes(1, rows)] + last[:, lanes(2, rows)]


def body(
    nt, ns, level, cur, ctx, cot, wf, wr, out, rg,
    flat, tctx, flag_s, flag_r, mctx, sel_o, sel_l, x_o, x_l, m_l, tcur, tcot, ccot,
    stack, stack_c, stack_g, stack_3, stack_4, p1_cur, g4_o, g4_e, p1_o, p1_e, d1, d2, d3_o, d3_e, outs,
    h1o_s, h1o_r, h1e_s, h1e_r, h3_s, h3_r, om_s, om_r, ox_s, ox_r, em_s, em_r, ex_s, ex_r, ey_r,
    w_fwd, w_bwd, w_ctx, w_back, ssem, rsem,
):
    tm = lax.axis_index("tm")
    sp = lax.axis_index("space")
    core = lax.rem(tm, 2)
    mate = tm + 1 - 2 * core
    cross = tm - 1 + 2 * core
    cross_ok = (cross >= 0) & (cross < nt)
    up_ok = sp < ns - 1
    dn_ok = sp > 0
    always = tm >= 0
    sent = {}
    left = set()
    g4, p1, d3, h1_s, h1_r = (g4_o, g4_e), (p1_o, p1_e), (d3_o, d3_e), (h1o_s, h1e_s), (h1o_r, h1e_r)

    def link(i, src, dst, device):
        return pltpu.make_async_remote_copy(
            src_ref=src, dst_ref=dst, send_sem=ssem.at[i], recv_sem=rsem.at[i],
            device_id=device, device_id_type=MESH,
        )

    def send(i, src, dst, device, ok, from_ok):
        @pl.when(ok)
        def _():
            link(i, src, dst, device).start()

        sent[i] = (src, dst, device, ok, from_ok)

    def arrive(*which):
        for i in which:
            src, dst, _, _, ok = sent[i]

            @pl.when(ok)
            def _():
                link(i, src, dst, (tm, sp)).wait_recv()

    def gone(*which):
        for i in which:
            src, dst, device, ok, _ = sent[i]
            left.add(i)

            @pl.when(ok)
            def _():
                link(i, src, dst, device).wait_send()

    partners = []
    for who, who_ok in ((mate, always), (cross, cross_ok)):
        partners.append((who, sp, who_ok))
        partners.append((who, sp + 1, who_ok & up_ok))
        partners.append((who, sp - 1, who_ok & dn_ok))
    partners.append((tm, sp + 1, up_ok))
    partners.append((tm, sp - 1, dn_ok))
    barrier = pltpu.get_barrier_semaphore()
    for a, b, ok in partners:
        @pl.when(ok)
        def _():
            pl.semaphore_signal(barrier, inc=1, device_id=(a, b), device_id_type=MESH)

    def rows_first(src, i, dst, row0):
        flat[...] = src[i].astype(F32).reshape(C * H, W)
        for r in range(H):
            dst[i, :, lanes(row0 + r, 1)] = flat[pl.ds(r, C, stride=H), :].astype(BF)

    has_l0 = level[0] == 1
    has_l1 = level[1] == 1
    has_l = has_l0 | has_l1
    flag_s[...] = jnp.full((16, W), jnp.where(has_l0, 1.0, 0.0), F32).astype(BF)
    for i in range(2):
        rows_first(ctx, i, tctx, 0)
    spans = 1 + up_ok.astype(jnp.int32) + dn_ok.astype(jnp.int32)
    pl.semaphore_wait(barrier, spans * (2 + cross_ok.astype(jnp.int32)) - 1)

    send(0, flag_s, flag_r, (mate, sp), always, always)
    send(1, tctx, mctx.at[:, :, lanes(1, H)], (mate, sp), always, always)
    send(2, tctx.at[:, :, lanes(H - 1, 1)], mctx.at[:, :, lanes(0, 1)], (mate, sp + 1), up_ok, dn_ok)
    send(3, tctx.at[:, :, lanes(0, 1)], mctx.at[:, :, lanes(H + 1, 1)], (mate, sp - 1), dn_ok, up_ok)
    for i in range(2):
        rows_first(cur, i, tcur, 1)
    send(4, tcur.at[:, :, lanes(H, 1)], tcur.at[:, :, lanes(0, 1)], (tm, sp + 1), up_ok, dn_ok)
    send(5, tcur.at[:, :, lanes(1, 1)], tcur.at[:, :, lanes(H + 1, 1)], (tm, sp - 1), dn_ok, up_ok)

    arrive(0)
    mate_l0 = jnp.broadcast_to(flag_r[0:1, :].astype(F32), (C, W))
    even0 = jnp.maximum(mate_l0, jnp.where(has_l0, 1.0, 0.0))

    def wide(n):
        return jnp.concatenate([even0] * n, axis=1) > 0.5

    def pick(which, zero, one):
        zero, one = zero.astype(F32), one.astype(F32)
        mask = wide(zero.shape[1] // W)
        return jnp.where(mask, zero, one) if which == EVEN else jnp.where(mask, one, zero)

    arrive(1)
    mate_even = pick(EVEN, mctx[0, :, lanes(1, H)], mctx[1, :, lanes(1, H)])
    sel_l[...] = jnp.where(has_l, pick(EVEN, tctx[0], tctx[1]), mate_even).astype(BF)
    send(9, sel_l, x_l.at[:, lanes(1, H)], (cross, sp), cross_ok, cross_ok)
    send(10, sel_l.at[:, lanes(H - 1, 1)], x_l.at[:, lanes(0, 1)], (cross, sp + 1), cross_ok & up_ok, cross_ok & dn_ok)
    send(11, sel_l.at[:, lanes(0, 1)], x_l.at[:, lanes(H + 1, 1)], (cross, sp - 1), cross_ok & dn_ok, cross_ok & up_ok)
    sel_o[...] = pick(ODD, tctx[0], tctx[1]).astype(BF)

    for i in range(2):
        rows_first(cot, i, tcot, 0)
    for c, halo in ((ODD, 5), (EVEN, 2)):
        ccot[c, :, lanes(5, H)] = pick(c, tcot[0], tcot[1]).astype(BF)
        top, bottom = lanes(5 - halo, halo), lanes(H + 5, halo)
        send(12 + 8 * c, ccot.at[c, :, lanes(H + 5 - halo, halo)], ccot.at[c, :, top], (tm, sp + 1), up_ok, dn_ok)
        send(13 + 8 * c, ccot.at[c, :, lanes(5, halo)], ccot.at[c, :, bottom], (tm, sp - 1), dn_ok, up_ok)

    def clear(ok, ref, where, lead):
        @pl.when(jnp.logical_not(ok))
        def _():
            for c in range(lead):
                view = ref.at[c] if lead > 1 else ref
                n = where.stop - where.start
                view[:, where] = jnp.zeros((C, n), BF)

    clear(dn_ok, tcur, lanes(0, 1), 2)
    clear(up_ok, tcur, lanes(H + 1, 1), 2)
    clear(dn_ok, ccot, lanes(0, 5), 2)
    clear(up_ok, ccot, lanes(H + 5, 5), 2)
    clear(dn_ok, mctx, lanes(0, 1), 2)
    clear(up_ok, mctx, lanes(H + 1, 1), 2)
    for ref in (x_o, x_l):
        clear(cross_ok, ref, lanes(1, H), 1)
        clear(cross_ok & dn_ok, ref, lanes(0, 1), 1)
        clear(cross_ok & up_ok, ref, lanes(H + 1, 1), 1)
    mate_cross = tm + 2 - 4 * core
    mate_cross_ok = (mate_cross >= 0) & (mate_cross < nt)
    clear(mate_cross_ok, m_l, lanes(0, H + 2), 1)
    for ref, n in ((h1o_r, 7), (h1e_r, 4), (h3_r, 3)):
        clear(dn_ok, ref.at[0], lanes(0, n), 1)
        clear(up_ok, ref.at[1], lanes(0, n), 1)
    clear(cross_ok, ox_r, lanes(0, H), 1)
    clear(cross_ok, ex_r, lanes(0, H), 1)
    clear(mate_cross_ok, ey_r, lanes(0, H), 1)

    eye_r = lax.broadcasted_iota(jnp.int32, (3 * C, 3 * C), 0)
    eye_c = lax.broadcasted_iota(jnp.int32, (3 * C, 3 * C), 1)
    eye = jnp.where(eye_r == eye_c, 1.0, 0.0).astype(BF)

    def turned(m):
        return lax.dot_general(
            eye[: m.shape[1], : m.shape[1]], m, (((1,), (1,)), ((), ())), preferred_element_type=F32
        ).astype(BF)

    for c in (ODD, EVEN):
        def first_tap(t):
            if c == ODD:
                return wf[1, t]
            return jnp.where(has_l, wf[0, t].astype(F32), wf[1, t].astype(F32)).astype(BF)

        def rest_tap(k, t):
            if c == ODD:
                return wr[1, k, t]
            return jnp.where(has_l, wr[0, k, t].astype(F32), wr[1, k, t].astype(F32)).astype(BF)

        taps = [first_tap(t) for t in range(9)]
        for g in range(3):
            part = [tap[:, g * C : (g + 1) * C] for tap in taps]
            for a in range(3):
                rows = jnp.concatenate(part[3 * a : 3 * a + 3], axis=1)
                if g == 0:
                    w_fwd[c, 0, a * C : (a + 1) * C, :] = rows
                else:
                    w_ctx[c, a * C : (a + 1) * C, (g - 1) * 3 * C : g * 3 * C] = rows
        both = [tap[:, C:] for tap in taps]
        for a in range(3):
            m = jnp.concatenate([both[3 * a + b] for b in range(3)], axis=0)
            w_back[c, a * 2 * C : (a + 1) * 2 * C, :] = turned(m)
        for k in range(4):
            part = [rest_tap(k, t) for t in range(9)]
            for a in range(3):
                w_fwd[c, k + 1, a * C : (a + 1) * C, :] = jnp.concatenate(part[3 * a : 3 * a + 3], axis=1)
                m = jnp.concatenate([part[3 * a + b] for b in range(3)], axis=0)
                w_bwd[c, k, a * C : (a + 1) * C, :] = turned(m)

    gone(9)
    send(6, sel_o, x_o.at[:, lanes(1, H)], (cross, sp), cross_ok, cross_ok)
    send(7, sel_o.at[:, lanes(H - 1, 1)], x_o.at[:, lanes(0, 1)], (cross, sp + 1), cross_ok & up_ok, cross_ok & dn_ok)
    send(8, sel_o.at[:, lanes(0, 1)], x_o.at[:, lanes(H + 1, 1)], (cross, sp - 1), cross_ok & dn_ok, cross_ok & up_ok)

    arrive(4)
    arrive(5)
    for c in (ODD, EVEN):
        put(stack, lanes(0, H + 2), pick(c, tcur[0], tcur[1]))
        p1_cur[c] = conv(w_fwd[c, 0], stack[:, lanes(0, H + 2)])
    for c, halo in ((EVEN, 2), (ODD, 5)):
        arrive(12 + 8 * c, 13 + 8 * c)
        rows = H + 2 * halo
        put(stack_g, lanes(0, rows), ccot[c, :, lanes(5 - halo, rows)].astype(F32), flip=True)
        g4[c][...] = conv(w_bwd[c, 3], stack_g[:, lanes(0, rows)], flip=True)

    arrive(2)
    arrive(3)
    first_core = core == 0
    reach = (7, 4)

    def layer_one(c, outer, inner):
        put(stack_c, lanes(0, H + 2), jnp.where(first_core, outer, inner))
        put(stack_c, lanes(0, H + 2), jnp.where(first_core, inner, outer), base=3 * C)
        pre = p1_cur[c] + conv(w_ctx[c], stack_c[...])
        halo = reach[c]
        p1[c][:, lanes(halo, H)] = pre
        h1_s[c][0] = pre[:, lanes(H - halo, halo)].astype(BF)
        h1_s[c][1] = pre[:, lanes(0, halo)].astype(BF)
        send(14 + 2 * c, h1_s[c].at[0], h1_r[c].at[0], (tm, sp + 1), up_ok, dn_ok)
        send(15 + 2 * c, h1_s[c].at[1], h1_r[c].at[1], (tm, sp - 1), dn_ok, up_ok)

    def activate(pre, halo):
        sigma = 1.0 / (1.0 + jnp.exp(-pre))
        act = pre * sigma
        slope = sigma * (1.0 + pre * (1.0 - sigma))
        row = (lax.broadcasted_iota(jnp.int32, pre.shape, 1) >> 7) + (sp * H - halo)
        inside = (row >= 0) & (row < ns * H)
        return jnp.where(inside, act, 0.0), jnp.where(inside, slope, 0.0)

    def forward(c):
        h = reach[c]
        arrive(14 + 2 * c, 15 + 2 * c)
        p1[c][:, lanes(0, h)] = h1_r[c][0].astype(F32)
        p1[c][:, lanes(H + h, h)] = h1_r[c][1].astype(F32)
        act, slope = activate(p1[c][...], h)
        d1[c] = slope[:, lanes(h - 1, H + 2)]
        for k in (1, 2, 3):
            rows = lanes(0, H + 2 * (h + 1 - k))
            put(stack, rows, act)
            act, slope = activate(conv(w_fwd[c, k], stack[:, rows]), h - k)
            if k == 1:
                d2[c] = slope[:, lanes(h - 3, H + 4)]
            if k == 2:
                d3[c][...] = slope[:, lanes(2, H + 2 * (h - 4))]
        rows = lanes(0, H + 2 * (h - 3))
        put(stack_g, rows, g4[c][...] * slope, flip=True)
        s3 = conv(w_bwd[c, 2], stack_g[:, rows], flip=True) * d3[c][...]
        if c == EVEN:
            h3_s[0] = s3[:, lanes(H - 3, 3)].astype(BF)
            h3_s[1] = s3[:, lanes(0, 3)].astype(BF)
            send(18, h3_s.at[0], h3_r.at[0], (tm, sp + 1), up_ok, dn_ok)
            send(19, h3_s.at[1], h3_r.at[1], (tm, sp - 1), dn_ok, up_ok)
        put(stack_3.at[c], lanes(7 - h, H + 2 * (h - 4)), s3, flip=True)
        put(stack_4.at[c], lanes(0, H + 2), act[:, lanes(h - 4, H + 2)])

    def finish(c):
        own = pick(c, tcur[0, :, lanes(1, H)], tcur[1, :, lanes(1, H)])
        outs[c] = own + conv(w_fwd[c, 4], stack_4[c])

    def backward(c):
        if c == EVEN:
            arrive(18, 19)
            put(stack_3.at[c], lanes(0, 3), h3_r[0].astype(F32), flip=True)
            put(stack_3.at[c], lanes(H + 3, 3), h3_r[1].astype(F32), flip=True)
        s2 = conv(w_bwd[c, 1], stack_3[c], flip=True) * d2[c]
        put(stack_g, lanes(0, 20), s2, flip=True)
        s1 = conv(w_bwd[c, 0], stack_g[:, lanes(0, 20)], flip=True) * d1[c]
        put(stack_g, lanes(0, 18), s1, flip=True)
        grads = conv(w_back[c], stack_g[:, lanes(0, 18)], flip=True, out_channels=2 * C)
        behind, ahead = grads[:C], grads[C:]
        return jnp.where(first_core, behind, ahead), jnp.where(first_core, ahead, behind)

    arrive(9, 10, 11)
    send(22, x_l, m_l, (mate, sp), cross_ok, mate_cross_ok)
    arrive(22)
    inner = jnp.where(has_l, m_l[...].astype(F32), pick(EVEN, mctx[0], mctx[1]))
    layer_one(EVEN, x_l[...].astype(F32), inner)
    forward(EVEN)
    arrive(6, 7, 8)
    layer_one(ODD, x_o[...].astype(F32), pick(ODD, mctx[0], mctx[1]))
    outer_g, inner_g = backward(EVEN)
    em_s[...] = inner_g.astype(BF)
    send(25, em_s, em_r, (mate, sp), always, always)
    finish(EVEN)
    arrive(25)
    from_mate = em_r[...].astype(F32)
    ex_s[...] = (outer_g + jnp.where(has_l, 0.0, from_mate)).astype(BF)
    send(26, ex_s, ex_r, (cross, sp), cross_ok, cross_ok)
    forward(ODD)
    outer_g, inner_g = backward(ODD)
    ox_s[...] = outer_g.astype(BF)
    send(23, ox_s, ox_r, (cross, sp), cross_ok, cross_ok)
    om_s[...] = inner_g.astype(BF)
    send(24, om_s, om_r, (mate, sp), always, always)
    finish(ODD)
    mask = wide(H)
    out[0] = jnp.where(mask, outs[EVEN], outs[ODD]).astype(BF)
    out[1] = jnp.where(mask, outs[ODD], outs[EVEN]).astype(BF)
    arrive(26)
    send(27, ex_r, ey_r, (mate, sp), cross_ok, mate_cross_ok)
    arrive(27)
    even_g = ex_r[...].astype(F32) + ey_r[...].astype(F32) + em_r[...].astype(F32)
    even_g = jnp.where(has_l, even_g, 0.0)
    arrive(24, 23)
    odd_g = ox_r[...].astype(F32) + om_r[...].astype(F32)
    rg[0] = jnp.where(mask, even_g, odd_g)
    rg[1] = jnp.where(mask, odd_g, even_g)
    gone(*(i for i in sent if i not in left))


def solution(mesh):
    nt, ns = mesh.shape["tm"], mesh.shape["space"]

    def on_device(current, contexts, cotangent, level_table, ref_table, w_first, w_rest):
        vmem = pl.BlockSpec(memory_space=pltpu.VMEM)

        def bf(*shape):
            return pltpu.VMEM(shape, BF)

        def f32(*shape):
            return pltpu.VMEM(shape, F32)

        slab = H * W
        halo = (H + 2) * W
        scratch = [
            f32(C * H, W), bf(2, C, slab), bf(16, W), bf(16, W), bf(2, C, halo), bf(C, slab), bf(C, slab),
            bf(C, halo), bf(C, halo), bf(C, halo), bf(2, C, halo), bf(2, C, slab), bf(2, C, (H + 10) * W),
            bf(3 * C, 30 * W), bf(6 * C, halo), bf(3 * C, 26 * W), bf(2, 3 * C, 22 * W), bf(2, 3 * C, halo),
            f32(2, C, slab), f32(C, 24 * W), f32(C, halo), f32(C, 30 * W), f32(C, 24 * W),
            f32(2, C, halo), f32(2, C, (H + 4) * W), f32(C, 22 * W), f32(C, slab), f32(2, C, slab),
            bf(2, C, 7 * W), bf(2, C, 7 * W), bf(2, C, 4 * W), bf(2, C, 4 * W), bf(2, C, 3 * W), bf(2, C, 3 * W),
            bf(C, slab), bf(C, slab), bf(C, slab), bf(C, slab),
            bf(C, slab), bf(C, slab), bf(C, slab), bf(C, slab), bf(C, slab),
            bf(2, 5, 3 * C, 3 * C), bf(2, 4, 3 * C, 3 * C), bf(2, 3 * C, 6 * C), bf(2, 6 * C, 3 * C),
            pltpu.SemaphoreType.DMA((28,)), pltpu.SemaphoreType.DMA((28,)),
        ]

        def kernel(*refs):
            body(nt, ns, *refs)

        out, rg = pl.pallas_call(
            kernel,
            out_shape=(
                jax.ShapeDtypeStruct((2, C, slab), BF),
                jax.ShapeDtypeStruct((2, C, slab), F32),
            ),
            in_specs=[pl.BlockSpec(memory_space=pltpu.SMEM)] + [vmem] * 5,
            out_specs=(vmem, vmem),
            scratch_shapes=scratch,
            compiler_params=pltpu.CompilerParams(
                collective_id=0, has_side_effects=True, vmem_limit_bytes=56 << 20
            ),
            name="coding",
        )(level_table, current, contexts, cotangent, w_first, w_rest)
        return out.reshape(2, C, H, W), rg.reshape(2, C, H, W)

    frames = P("tm", None, "space", None)
    return jax.shard_map(
        on_device,
        mesh=mesh,
        in_specs=(frames, frames, frames, P("tm"), P("tm", None), P(), P()),
        out_specs=(frames, frames),
        check_vma=False,
    )
```

```python
import jax
import jax.numpy as jnp
from jax import lax
from jax.experimental import pallas as pl
from jax.experimental.pallas import tpu as pltpu
from jax.sharding import PartitionSpec as P

MESH = pl.DeviceIdType.MESH
F32 = jnp.float32
BF = jnp.bfloat16
C = 64
W = 128
H = 16
ODD, EVEN = 0, 1


def lanes(start, count):
    return slice(start * W, (start + count) * W)


def shifted(a):
    n = a.shape[1]
    lane = lax.broadcasted_iota(jnp.int32, a.shape, 1) & (W - 1)
    left = jnp.where(lane == 0, 0.0, pltpu.roll(a, 1, 1))
    right = jnp.where(lane == W - 1, 0.0, pltpu.roll(a, n - 1, 1))
    return left, right


def put(ref, where, a, flip=False, base=0):
    left, right = shifted(a)
    first, last = (right, left) if flip else (left, right)
    ref[base : base + C, where] = first.astype(BF)
    ref[base + C : base + 2 * C, where] = a.astype(BF)
    ref[base + 2 * C : base + 3 * C, where] = last.astype(BF)


def conv(weights, stack, flip=False, out_channels=C):
    t = jnp.dot(weights, stack, preferred_element_type=F32)
    rows = stack.shape[1] // W - 2
    o = out_channels
    first, last = (t[2 * o : 3 * o], t[0:o]) if flip else (t[0:o], t[2 * o : 3 * o])
    return first[:, lanes(0, rows)] + t[o : 2 * o, lanes(1, rows)] + last[:, lanes(2, rows)]


def body(
    nt, ns, level, cur_in, ctx_in, cot_in, wf_in, wr_in, out, rg,
    cur, ctx, cot, wf, wr,
    flat, tctx, flag_s, flag_r, mctx, sel_o, sel_l, x_o, x_l, m_l, tcur, tcot, ccot,
    stack, stack_c, stack_g, stack_3, stack_4, p1_cur, g4_o, g4_e, p1_o, p1_e, d1, d2, d3_o, d3_e, outs,
    h1o_s, h1o_r, h1e_s, h1e_r, h3_s, h3_r, om_s, om_r, ox_s, ox_r, em_s, em_r, ex_s, ex_r, ey_r,
    w_fwd, w_bwd, w_ctx, w_back, ssem, rsem, lsem,
):
    tm = lax.axis_index("tm")
    sp = lax.axis_index("space")
    core = lax.rem(tm, 2)
    mate = tm + 1 - 2 * core
    cross = tm - 1 + 2 * core
    cross_ok = (cross >= 0) & (cross < nt)
    up_ok = sp < ns - 1
    dn_ok = sp > 0
    always = tm >= 0
    sent = {}
    left = set()
    g4, p1, d3, h1_s, h1_r = (g4_o, g4_e), (p1_o, p1_e), (d3_o, d3_e), (h1o_s, h1e_s), (h1o_r, h1e_r)

    def link(i, src, dst, device):
        return pltpu.make_async_remote_copy(
            src_ref=src, dst_ref=dst, send_sem=ssem.at[i], recv_sem=rsem.at[i],
            device_id=device, device_id_type=MESH,
        )

    def send(i, src, dst, device, ok, from_ok):
        @pl.when(ok)
        def _():
            link(i, src, dst, device).start()

        sent[i] = (src, dst, device, ok, from_ok)

    def arrive(*which):
        for i in which:
            src, dst, _, _, ok = sent[i]

            @pl.when(ok)
            def _():
                link(i, src, dst, (tm, sp)).wait_recv()

    def gone(*which):
        for i in which:
            src, dst, device, ok, _ = sent[i]
            left.add(i)

            @pl.when(ok)
            def _():
                link(i, src, dst, device).wait_send()

    partners = []
    for who, who_ok in ((mate, always), (cross, cross_ok)):
        partners.append((who, sp, who_ok))
        partners.append((who, sp + 1, who_ok & up_ok))
        partners.append((who, sp - 1, who_ok & dn_ok))
    partners.append((tm, sp + 1, up_ok))
    partners.append((tm, sp - 1, dn_ok))
    barrier = pltpu.get_barrier_semaphore()
    for a, b, ok in partners:
        @pl.when(ok)
        def _():
            pl.semaphore_signal(barrier, inc=1, device_id=(a, b), device_id_type=MESH)

    loads = [
        pltpu.make_async_copy(src, dst, lsem.at[i])
        for i, (src, dst) in enumerate(((ctx_in, ctx), (cur_in, cur), (cot_in, cot), (wf_in, wf), (wr_in, wr)))
    ]
    for load in loads:
        load.start()

    def rows_first(src, i, dst, row0):
        flat[...] = src[i].astype(F32).reshape(C * H, W)
        for r in range(H):
            dst[i, :, lanes(row0 + r, 1)] = flat[pl.ds(r, C, stride=H), :].astype(BF)

    has_l0 = level[0] == 1
    has_l1 = level[1] == 1
    has_l = has_l0 | has_l1
    flag_s[...] = jnp.full((16, W), jnp.where(has_l0, 1.0, 0.0), F32).astype(BF)
    loads[0].wait()
    for i in range(2):
        rows_first(ctx, i, tctx, 0)
    spans = 1 + up_ok.astype(jnp.int32) + dn_ok.astype(jnp.int32)
    pl.semaphore_wait(barrier, spans * (2 + cross_ok.astype(jnp.int32)) - 1)

    send(0, flag_s, flag_r, (mate, sp), always, always)
    send(1, tctx, mctx.at[:, :, lanes(1, H)], (mate, sp), always, always)
    send(2, tctx.at[:, :, lanes(H - 1, 1)], mctx.at[:, :, lanes(0, 1)], (mate, sp + 1), up_ok, dn_ok)
    send(3, tctx.at[:, :, lanes(0, 1)], mctx.at[:, :, lanes(H + 1, 1)], (mate, sp - 1), dn_ok, up_ok)
    loads[1].wait()
    for i in range(2):
        rows_first(cur, i, tcur, 1)
    send(4, tcur.at[:, :, lanes(H, 1)], tcur.at[:, :, lanes(0, 1)], (tm, sp + 1), up_ok, dn_ok)
    send(5, tcur.at[:, :, lanes(1, 1)], tcur.at[:, :, lanes(H + 1, 1)], (tm, sp - 1), dn_ok, up_ok)

    arrive(0)
    mate_l0 = jnp.broadcast_to(flag_r[0:1, :].astype(F32), (C, W))
    even0 = jnp.maximum(mate_l0, jnp.where(has_l0, 1.0, 0.0))

    def wide(n):
        return jnp.concatenate([even0] * n, axis=1) > 0.5

    def pick(which, zero, one):
        zero, one = zero.astype(F32), one.astype(F32)
        mask = wide(zero.shape[1] // W)
        return jnp.where(mask, zero, one) if which == EVEN else jnp.where(mask, one, zero)

    arrive(1)
    mate_even = pick(EVEN, mctx[0, :, lanes(1, H)], mctx[1, :, lanes(1, H)])
    sel_l[...] = jnp.where(has_l, pick(EVEN, tctx[0], tctx[1]), mate_even).astype(BF)
    send(9, sel_l, x_l.at[:, lanes(1, H)], (cross, sp), cross_ok, cross_ok)
    send(10, sel_l.at[:, lanes(H - 1, 1)], x_l.at[:, lanes(0, 1)], (cross, sp + 1), cross_ok & up_ok, cross_ok & dn_ok)
    send(11, sel_l.at[:, lanes(0, 1)], x_l.at[:, lanes(H + 1, 1)], (cross, sp - 1), cross_ok & dn_ok, cross_ok & up_ok)
    sel_o[...] = pick(ODD, tctx[0], tctx[1]).astype(BF)

    loads[2].wait()
    for i in range(2):
        rows_first(cot, i, tcot, 0)
    for c, halo in ((ODD, 5), (EVEN, 2)):
        ccot[c, :, lanes(5, H)] = pick(c, tcot[0], tcot[1]).astype(BF)
        top, bottom = lanes(5 - halo, halo), lanes(H + 5, halo)
        send(12 + 8 * c, ccot.at[c, :, lanes(H + 5 - halo, halo)], ccot.at[c, :, top], (tm, sp + 1), up_ok, dn_ok)
        send(13 + 8 * c, ccot.at[c, :, lanes(5, halo)], ccot.at[c, :, bottom], (tm, sp - 1), dn_ok, up_ok)

    def clear(ok, ref, where, lead):
        @pl.when(jnp.logical_not(ok))
        def _():
            for c in range(lead):
                view = ref.at[c] if lead > 1 else ref
                n = where.stop - where.start
                view[:, where] = jnp.zeros((C, n), BF)

    clear(dn_ok, tcur, lanes(0, 1), 2)
    clear(up_ok, tcur, lanes(H + 1, 1), 2)
    clear(dn_ok, ccot, lanes(0, 5), 2)
    clear(up_ok, ccot, lanes(H + 5, 5), 2)
    clear(dn_ok, mctx, lanes(0, 1), 2)
    clear(up_ok, mctx, lanes(H + 1, 1), 2)
    for ref in (x_o, x_l):
        clear(cross_ok, ref, lanes(1, H), 1)
        clear(cross_ok & dn_ok, ref, lanes(0, 1), 1)
        clear(cross_ok & up_ok, ref, lanes(H + 1, 1), 1)
    mate_cross = tm + 2 - 4 * core
    mate_cross_ok = (mate_cross >= 0) & (mate_cross < nt)
    clear(mate_cross_ok, m_l, lanes(0, H + 2), 1)
    for ref, n in ((h1o_r, 7), (h1e_r, 4), (h3_r, 3)):
        clear(dn_ok, ref.at[0], lanes(0, n), 1)
        clear(up_ok, ref.at[1], lanes(0, n), 1)
    clear(cross_ok, ox_r, lanes(0, H), 1)
    clear(cross_ok, ex_r, lanes(0, H), 1)
    clear(mate_cross_ok, ey_r, lanes(0, H), 1)

    loads[3].wait()
    loads[4].wait()
    eye_r = lax.broadcasted_iota(jnp.int32, (3 * C, 3 * C), 0)
    eye_c = lax.broadcasted_iota(jnp.int32, (3 * C, 3 * C), 1)
    eye = jnp.where(eye_r == eye_c, 1.0, 0.0).astype(BF)

    def turned(m):
        return lax.dot_general(
            eye[: m.shape[1], : m.shape[1]], m, (((1,), (1,)), ((), ())), preferred_element_type=F32
        ).astype(BF)

    for c in (ODD, EVEN):
        def first_tap(t):
            if c == ODD:
                return wf[1, t]
            return jnp.where(has_l, wf[0, t].astype(F32), wf[1, t].astype(F32)).astype(BF)

        def rest_tap(k, t):
            if c == ODD:
                return wr[1, k, t]
            return jnp.where(has_l, wr[0, k, t].astype(F32), wr[1, k, t].astype(F32)).astype(BF)

        taps = [first_tap(t) for t in range(9)]
        for g in range(3):
            part = [tap[:, g * C : (g + 1) * C] for tap in taps]
            for a in range(3):
                rows = jnp.concatenate(part[3 * a : 3 * a + 3], axis=1)
                if g == 0:
                    w_fwd[c, 0, a * C : (a + 1) * C, :] = rows
                else:
                    w_ctx[c, a * C : (a + 1) * C, (g - 1) * 3 * C : g * 3 * C] = rows
        both = [tap[:, C:] for tap in taps]
        for a in range(3):
            m = jnp.concatenate([both[3 * a + b] for b in range(3)], axis=0)
            w_back[c, a * 2 * C : (a + 1) * 2 * C, :] = turned(m)
        for k in range(4):
            part = [rest_tap(k, t) for t in range(9)]
            for a in range(3):
                w_fwd[c, k + 1, a * C : (a + 1) * C, :] = jnp.concatenate(part[3 * a : 3 * a + 3], axis=1)
                m = jnp.concatenate([part[3 * a + b] for b in range(3)], axis=0)
                w_bwd[c, k, a * C : (a + 1) * C, :] = turned(m)

    gone(9)
    send(6, sel_o, x_o.at[:, lanes(1, H)], (cross, sp), cross_ok, cross_ok)
    send(7, sel_o.at[:, lanes(H - 1, 1)], x_o.at[:, lanes(0, 1)], (cross, sp + 1), cross_ok & up_ok, cross_ok & dn_ok)
    send(8, sel_o.at[:, lanes(0, 1)], x_o.at[:, lanes(H + 1, 1)], (cross, sp - 1), cross_ok & dn_ok, cross_ok & up_ok)

    arrive(4)
    arrive(5)
    for c in (ODD, EVEN):
        put(stack, lanes(0, H + 2), pick(c, tcur[0], tcur[1]))
        p1_cur[c] = conv(w_fwd[c, 0], stack[:, lanes(0, H + 2)])
    for c, halo in ((EVEN, 2), (ODD, 5)):
        arrive(12 + 8 * c, 13 + 8 * c)
        rows = H + 2 * halo
        put(stack_g, lanes(0, rows), ccot[c, :, lanes(5 - halo, rows)].astype(F32), flip=True)
        g4[c][...] = conv(w_bwd[c, 3], stack_g[:, lanes(0, rows)], flip=True)

    arrive(2)
    arrive(3)
    first_core = core == 0
    reach = (7, 4)

    def layer_one(c, outer, inner):
        put(stack_c, lanes(0, H + 2), jnp.where(first_core, outer, inner))
        put(stack_c, lanes(0, H + 2), jnp.where(first_core, inner, outer), base=3 * C)
        pre = p1_cur[c] + conv(w_ctx[c], stack_c[...])
        halo = reach[c]
        p1[c][:, lanes(halo, H)] = pre
        h1_s[c][0] = pre[:, lanes(H - halo, halo)].astype(BF)
        h1_s[c][1] = pre[:, lanes(0, halo)].astype(BF)
        send(14 + 2 * c, h1_s[c].at[0], h1_r[c].at[0], (tm, sp + 1), up_ok, dn_ok)
        send(15 + 2 * c, h1_s[c].at[1], h1_r[c].at[1], (tm, sp - 1), dn_ok, up_ok)

    def activate(pre, halo):
        sigma = 1.0 / (1.0 + jnp.exp(-pre))
        act = pre * sigma
        slope = sigma * (1.0 + pre * (1.0 - sigma))
        row = (lax.broadcasted_iota(jnp.int32, pre.shape, 1) >> 7) + (sp * H - halo)
        inside = (row >= 0) & (row < ns * H)
        return jnp.where(inside, act, 0.0), jnp.where(inside, slope, 0.0)

    def forward(c):
        h = reach[c]
        arrive(14 + 2 * c, 15 + 2 * c)
        p1[c][:, lanes(0, h)] = h1_r[c][0].astype(F32)
        p1[c][:, lanes(H + h, h)] = h1_r[c][1].astype(F32)
        act, slope = activate(p1[c][...], h)
        d1[c] = slope[:, lanes(h - 1, H + 2)]
        for k in (1, 2, 3):
            rows = lanes(0, H + 2 * (h + 1 - k))
            put(stack, rows, act)
            act, slope = activate(conv(w_fwd[c, k], stack[:, rows]), h - k)
            if k == 1:
                d2[c] = slope[:, lanes(h - 3, H + 4)]
            if k == 2:
                d3[c][...] = slope[:, lanes(2, H + 2 * (h - 4))]
        rows = lanes(0, H + 2 * (h - 3))
        put(stack_g, rows, g4[c][...] * slope, flip=True)
        s3 = conv(w_bwd[c, 2], stack_g[:, rows], flip=True) * d3[c][...]
        if c == EVEN:
            h3_s[0] = s3[:, lanes(H - 3, 3)].astype(BF)
            h3_s[1] = s3[:, lanes(0, 3)].astype(BF)
            send(18, h3_s.at[0], h3_r.at[0], (tm, sp + 1), up_ok, dn_ok)
            send(19, h3_s.at[1], h3_r.at[1], (tm, sp - 1), dn_ok, up_ok)
        put(stack_3.at[c], lanes(7 - h, H + 2 * (h - 4)), s3, flip=True)
        put(stack_4.at[c], lanes(0, H + 2), act[:, lanes(h - 4, H + 2)])

    def finish(c):
        own = pick(c, tcur[0, :, lanes(1, H)], tcur[1, :, lanes(1, H)])
        outs[c] = own + conv(w_fwd[c, 4], stack_4[c])

    def backward(c):
        if c == EVEN:
            arrive(18, 19)
            put(stack_3.at[c], lanes(0, 3), h3_r[0].astype(F32), flip=True)
            put(stack_3.at[c], lanes(H + 3, 3), h3_r[1].astype(F32), flip=True)
        s2 = conv(w_bwd[c, 1], stack_3[c], flip=True) * d2[c]
        put(stack_g, lanes(0, 20), s2, flip=True)
        s1 = conv(w_bwd[c, 0], stack_g[:, lanes(0, 20)], flip=True) * d1[c]
        put(stack_g, lanes(0, 18), s1, flip=True)
        grads = conv(w_back[c], stack_g[:, lanes(0, 18)], flip=True, out_channels=2 * C)
        behind, ahead = grads[:C], grads[C:]
        return jnp.where(first_core, behind, ahead), jnp.where(first_core, ahead, behind)

    arrive(9, 10, 11)
    send(22, x_l, m_l, (mate, sp), cross_ok, mate_cross_ok)
    arrive(22)
    inner = jnp.where(has_l, m_l[...].astype(F32), pick(EVEN, mctx[0], mctx[1]))
    layer_one(EVEN, x_l[...].astype(F32), inner)
    arrive(6, 7, 8)
    layer_one(ODD, x_o[...].astype(F32), pick(ODD, mctx[0], mctx[1]))
    forward(EVEN)
    outer_g, inner_g = backward(EVEN)
    em_s[...] = inner_g.astype(BF)
    send(25, em_s, em_r, (mate, sp), always, always)
    finish(EVEN)
    arrive(25)
    from_mate = em_r[...].astype(F32)
    ex_s[...] = (outer_g + jnp.where(has_l, 0.0, from_mate)).astype(BF)
    send(26, ex_s, ex_r, (cross, sp), cross_ok, cross_ok)
    forward(ODD)
    outer_g, inner_g = backward(ODD)
    ox_s[...] = outer_g.astype(BF)
    send(23, ox_s, ox_r, (cross, sp), cross_ok, cross_ok)
    om_s[...] = inner_g.astype(BF)
    send(24, om_s, om_r, (mate, sp), always, always)
    finish(ODD)
    mask = wide(H)

    def channels_first(dst, i, value):
        for r in range(H):
            flat[pl.ds(r, C, stride=H), :] = value[:, lanes(r, 1)]
        dst[i] = flat[...].reshape(C, H, W).astype(dst.dtype)

    channels_first(out, 0, jnp.where(mask, outs[EVEN], outs[ODD]))
    channels_first(out, 1, jnp.where(mask, outs[ODD], outs[EVEN]))
    arrive(26)
    send(27, ex_r, ey_r, (mate, sp), cross_ok, mate_cross_ok)
    arrive(27)
    even_g = ex_r[...].astype(F32) + ey_r[...].astype(F32) + em_r[...].astype(F32)
    even_g = jnp.where(has_l, even_g, 0.0)
    arrive(24, 23)
    odd_g = ox_r[...].astype(F32) + om_r[...].astype(F32)
    channels_first(rg, 0, jnp.where(mask, even_g, odd_g))
    channels_first(rg, 1, jnp.where(mask, odd_g, even_g))
    gone(*(i for i in sent if i not in left))


def solution(mesh):
    nt, ns = mesh.shape["tm"], mesh.shape["space"]

    def on_device(current, contexts, cotangent, level_table, ref_table, w_first, w_rest):
        vmem = pl.BlockSpec(memory_space=pltpu.VMEM)

        def bf(*shape):
            return pltpu.VMEM(shape, BF)

        def f32(*shape):
            return pltpu.VMEM(shape, F32)

        slab = H * W
        halo = (H + 2) * W
        scratch = [
            bf(2, C, H, W), bf(2, C, H, W), bf(2, C, H, W), bf(2, 9, C, 3 * C), bf(2, 4, 9, C, C),
            f32(C * H, W), bf(2, C, slab), bf(16, W), bf(16, W), bf(2, C, halo), bf(C, slab), bf(C, slab),
            bf(C, halo), bf(C, halo), bf(C, halo), bf(2, C, halo), bf(2, C, slab), bf(2, C, (H + 10) * W),
            bf(3 * C, 30 * W), bf(6 * C, halo), bf(3 * C, 26 * W), bf(2, 3 * C, 22 * W), bf(2, 3 * C, halo),
            f32(2, C, slab), f32(C, 24 * W), f32(C, halo), f32(C, 30 * W), f32(C, 24 * W),
            f32(2, C, halo), f32(2, C, (H + 4) * W), f32(C, 22 * W), f32(C, slab), f32(2, C, slab),
            bf(2, C, 7 * W), bf(2, C, 7 * W), bf(2, C, 4 * W), bf(2, C, 4 * W), bf(2, C, 3 * W), bf(2, C, 3 * W),
            bf(C, slab), bf(C, slab), bf(C, slab), bf(C, slab),
            bf(C, slab), bf(C, slab), bf(C, slab), bf(C, slab), bf(C, slab),
            bf(2, 5, 3 * C, 3 * C), bf(2, 4, 3 * C, 3 * C), bf(2, 3 * C, 6 * C), bf(2, 6 * C, 3 * C),
            pltpu.SemaphoreType.DMA((29,)), pltpu.SemaphoreType.DMA((29,)), pltpu.SemaphoreType.DMA((5,)),
        ]

        def kernel(*refs):
            body(nt, ns, *refs)

        return pl.pallas_call(
            kernel,
            out_shape=(
                jax.ShapeDtypeStruct((2, C, H, W), BF),
                jax.ShapeDtypeStruct((2, C, H, W), F32),
            ),
            in_specs=[pl.BlockSpec(memory_space=pltpu.SMEM)] + [pl.BlockSpec(memory_space=pl.ANY)] * 5,
            out_specs=(vmem, vmem),
            scratch_shapes=scratch,
            compiler_params=pltpu.CompilerParams(
                collective_id=0, has_side_effects=True, vmem_limit_bytes=56 << 20
            ),
            name="coding",
        )(level_table, current, contexts, cotangent, w_first, w_rest)

    frames = P("tm", None, "space", None)
    return jax.shard_map(
        on_device,
        mesh=mesh,
        in_specs=(frames, frames, frames, P("tm"), P("tm", None), P(), P()),
        out_specs=(frames, frames),
        check_vma=False,
    )
```

```python
import jax
import jax.numpy as jnp
from jax import lax
from jax.experimental import pallas as pl
from jax.experimental.pallas import tpu as pltpu
from jax.sharding import PartitionSpec as P

MESH = pl.DeviceIdType.MESH
F32 = jnp.float32
BF = jnp.bfloat16
C = 64
W = 128
H = 16
ODD, EVEN = 0, 1


def lanes(start, count):
    return slice(start * W, (start + count) * W)


def shifted(a):
    n = a.shape[1]
    lane = lax.broadcasted_iota(jnp.int32, a.shape, 1) & (W - 1)
    left = jnp.where(lane == 0, 0.0, pltpu.roll(a, 1, 1))
    right = jnp.where(lane == W - 1, 0.0, pltpu.roll(a, n - 1, 1))
    return left, right


def put(ref, where, a, flip=False, base=0):
    left, right = shifted(a)
    first, last = (right, left) if flip else (left, right)
    ref[base : base + C, where] = first.astype(BF)
    ref[base + C : base + 2 * C, where] = a.astype(BF)
    ref[base + 2 * C : base + 3 * C, where] = last.astype(BF)


def conv(weights, stack, flip=False, out_channels=C):
    t = jnp.dot(weights, stack, preferred_element_type=F32)
    rows = stack.shape[1] // W - 2
    o = out_channels
    first, last = (t[2 * o : 3 * o], t[0:o]) if flip else (t[0:o], t[2 * o : 3 * o])
    return first[:, lanes(0, rows)] + t[o : 2 * o, lanes(1, rows)] + last[:, lanes(2, rows)]


def body(
    nt, ns, level, cur_in, ctx_in, cot_in, wf_in, wr_in, out, rg,
    cur, ctx, cot, wf, wr,
    flat, tctx, flag_s, flag_r, mctx, sel_o, sel_l, x_o, x_l, m_l, tcur, tcot, ccot,
    stack, stack_c, stack_g, stack_3, stack_4, p1_cur, g4_o, g4_e, p1_o, p1_e, d1, d2, d3_o, d3_e, outs,
    h1o_s, h1o_r, h1e_s, h1e_r, h3_s, h3_r, om_s, om_r, ox_s, ox_r, em_s, em_r, ex_s, ex_r, ey_r,
    w_fwd, w_bwd, w_ctx, w_back, ssem, rsem, lsem,
):
    tm = lax.axis_index("tm")
    sp = lax.axis_index("space")
    core = lax.rem(tm, 2)
    mate = tm + 1 - 2 * core
    cross = tm - 1 + 2 * core
    cross_ok = (cross >= 0) & (cross < nt)
    up_ok = sp < ns - 1
    dn_ok = sp > 0
    always = tm >= 0
    sent = {}
    left = set()
    g4, p1, d3, h1_s, h1_r = (g4_o, g4_e), (p1_o, p1_e), (d3_o, d3_e), (h1o_s, h1e_s), (h1o_r, h1e_r)

    def link(i, src, dst, device):
        return pltpu.make_async_remote_copy(
            src_ref=src, dst_ref=dst, send_sem=ssem.at[i], recv_sem=rsem.at[i],
            device_id=device, device_id_type=MESH,
        )

    def send(i, src, dst, device, ok, from_ok):
        @pl.when(ok)
        def _():
            link(i, src, dst, device).start()

        sent[i] = (src, dst, device, ok, from_ok)

    def arrive(*which):
        for i in which:
            src, dst, _, _, ok = sent[i]

            @pl.when(ok)
            def _():
                link(i, src, dst, (tm, sp)).wait_recv()

    def gone(*which):
        for i in which:
            src, dst, device, ok, _ = sent[i]
            left.add(i)

            @pl.when(ok)
            def _():
                link(i, src, dst, device).wait_send()

    partners = []
    for who, who_ok in ((mate, always), (cross, cross_ok)):
        partners.append((who, sp, who_ok))
        partners.append((who, sp + 1, who_ok & up_ok))
        partners.append((who, sp - 1, who_ok & dn_ok))
    partners.append((tm, sp + 1, up_ok))
    partners.append((tm, sp - 1, dn_ok))
    barrier = pltpu.get_barrier_semaphore()
    for a, b, ok in partners:
        @pl.when(ok)
        def _():
            pl.semaphore_signal(barrier, inc=1, device_id=(a, b), device_id_type=MESH)

    loads = [
        pltpu.make_async_copy(src, dst, lsem.at[i])
        for i, (src, dst) in enumerate(((ctx_in, ctx), (cur_in, cur), (cot_in, cot), (wf_in, wf), (wr_in, wr)))
    ]
    for load in loads:
        load.start()

    def rows_first(src, i, dst, row0):
        flat[...] = src[i].astype(F32).reshape(C * H, W)
        for r in range(H):
            dst[i, :, lanes(row0 + r, 1)] = flat[pl.ds(r, C, stride=H), :].astype(BF)

    has_l0 = level[0] == 1
    has_l1 = level[1] == 1
    has_l = has_l0 | has_l1
    flag_s[...] = jnp.full((16, W), jnp.where(has_l0, 1.0, 0.0), F32).astype(BF)
    loads[0].wait()
    for i in range(2):
        rows_first(ctx, i, tctx, 0)
    spans = 1 + up_ok.astype(jnp.int32) + dn_ok.astype(jnp.int32)
    pl.semaphore_wait(barrier, spans * (2 + cross_ok.astype(jnp.int32)) - 1)

    send(0, flag_s, flag_r, (mate, sp), always, always)
    send(1, tctx, mctx.at[:, :, lanes(1, H)], (mate, sp), always, always)
    send(2, tctx.at[:, :, lanes(H - 1, 1)], mctx.at[:, :, lanes(0, 1)], (mate, sp + 1), up_ok, dn_ok)
    send(3, tctx.at[:, :, lanes(0, 1)], mctx.at[:, :, lanes(H + 1, 1)], (mate, sp - 1), dn_ok, up_ok)
    loads[1].wait()
    for i in range(2):
        rows_first(cur, i, tcur, 1)
    send(4, tcur.at[:, :, lanes(H, 1)], tcur.at[:, :, lanes(0, 1)], (tm, sp + 1), up_ok, dn_ok)
    send(5, tcur.at[:, :, lanes(1, 1)], tcur.at[:, :, lanes(H + 1, 1)], (tm, sp - 1), dn_ok, up_ok)

    arrive(0)
    mate_l0 = jnp.broadcast_to(flag_r[0:1, :].astype(F32), (C, W))
    even0 = jnp.maximum(mate_l0, jnp.where(has_l0, 1.0, 0.0))

    def wide(n):
        return jnp.concatenate([even0] * n, axis=1) > 0.5

    def pick(which, zero, one):
        zero, one = zero.astype(F32), one.astype(F32)
        mask = wide(zero.shape[1] // W)
        return jnp.where(mask, zero, one) if which == EVEN else jnp.where(mask, one, zero)

    arrive(1)
    mate_even = pick(EVEN, mctx[0, :, lanes(1, H)], mctx[1, :, lanes(1, H)])
    sel_l[...] = jnp.where(has_l, pick(EVEN, tctx[0], tctx[1]), mate_even).astype(BF)
    send(9, sel_l, x_l.at[:, lanes(1, H)], (cross, sp), cross_ok, cross_ok)
    send(10, sel_l.at[:, lanes(H - 1, 1)], x_l.at[:, lanes(0, 1)], (cross, sp + 1), cross_ok & up_ok, cross_ok & dn_ok)
    send(11, sel_l.at[:, lanes(0, 1)], x_l.at[:, lanes(H + 1, 1)], (cross, sp - 1), cross_ok & dn_ok, cross_ok & up_ok)
    sel_o[...] = pick(ODD, tctx[0], tctx[1]).astype(BF)

    loads[2].wait()
    for i in range(2):
        rows_first(cot, i, tcot, 0)
    for c, halo in ((ODD, 5), (EVEN, 2)):
        ccot[c, :, lanes(5, H)] = pick(c, tcot[0], tcot[1]).astype(BF)
        top, bottom = lanes(5 - halo, halo), lanes(H + 5, halo)
        send(12 + 8 * c, ccot.at[c, :, lanes(H + 5 - halo, halo)], ccot.at[c, :, top], (tm, sp + 1), up_ok, dn_ok)
        send(13 + 8 * c, ccot.at[c, :, lanes(5, halo)], ccot.at[c, :, bottom], (tm, sp - 1), dn_ok, up_ok)

    def clear(ok, ref, where, lead):
        @pl.when(jnp.logical_not(ok))
        def _():
            for c in range(lead):
                view = ref.at[c] if lead > 1 else ref
                n = where.stop - where.start
                view[:, where] = jnp.zeros((C, n), BF)

    clear(dn_ok, tcur, lanes(0, 1), 2)
    clear(up_ok, tcur, lanes(H + 1, 1), 2)
    clear(dn_ok, ccot, lanes(0, 5), 2)
    clear(up_ok, ccot, lanes(H + 5, 5), 2)
    clear(dn_ok, mctx, lanes(0, 1), 2)
    clear(up_ok, mctx, lanes(H + 1, 1), 2)
    for ref in (x_o, x_l):
        clear(cross_ok, ref, lanes(1, H), 1)
        clear(cross_ok & dn_ok, ref, lanes(0, 1), 1)
        clear(cross_ok & up_ok, ref, lanes(H + 1, 1), 1)
    mate_cross = tm + 2 - 4 * core
    mate_cross_ok = (mate_cross >= 0) & (mate_cross < nt)
    clear(mate_cross_ok, m_l, lanes(0, H + 2), 1)
    for ref, n in ((h1o_r, 7), (h1e_r, 4), (h3_r, 3)):
        clear(dn_ok, ref.at[0], lanes(0, n), 1)
        clear(up_ok, ref.at[1], lanes(0, n), 1)
    clear(cross_ok, ox_r, lanes(0, H), 1)
    clear(cross_ok, ex_r, lanes(0, H), 1)
    clear(mate_cross_ok, ey_r, lanes(0, H), 1)

    loads[3].wait()
    loads[4].wait()
    eye_r = lax.broadcasted_iota(jnp.int32, (3 * C, 3 * C), 0)
    eye_c = lax.broadcasted_iota(jnp.int32, (3 * C, 3 * C), 1)
    eye = jnp.where(eye_r == eye_c, 1.0, 0.0).astype(BF)

    def turned(m):
        return lax.dot_general(
            eye[: m.shape[1], : m.shape[1]], m, (((1,), (1,)), ((), ())), preferred_element_type=F32
        ).astype(BF)

    for c in (ODD, EVEN):
        def first_tap(t):
            if c == ODD:
                return wf[1, t]
            return jnp.where(has_l, wf[0, t].astype(F32), wf[1, t].astype(F32)).astype(BF)

        def rest_tap(k, t):
            if c == ODD:
                return wr[1, k, t]
            return jnp.where(has_l, wr[0, k, t].astype(F32), wr[1, k, t].astype(F32)).astype(BF)

        taps = [first_tap(t) for t in range(9)]
        for g in range(3):
            part = [tap[:, g * C : (g + 1) * C] for tap in taps]
            for a in range(3):
                rows = jnp.concatenate(part[3 * a : 3 * a + 3], axis=1)
                if g == 0:
                    w_fwd[c, 0, a * C : (a + 1) * C, :] = rows
                else:
                    w_ctx[c, a * C : (a + 1) * C, (g - 1) * 3 * C : g * 3 * C] = rows
        both = [tap[:, C:] for tap in taps]
        for a in range(3):
            m = jnp.concatenate([both[3 * a + b] for b in range(3)], axis=0)
            w_back[c, a * 2 * C : (a + 1) * 2 * C, :] = turned(m)
        for k in range(4):
            part = [rest_tap(k, t) for t in range(9)]
            for a in range(3):
                w_fwd[c, k + 1, a * C : (a + 1) * C, :] = jnp.concatenate(part[3 * a : 3 * a + 3], axis=1)
                m = jnp.concatenate([part[3 * a + b] for b in range(3)], axis=0)
                w_bwd[c, k, a * C : (a + 1) * C, :] = turned(m)

    gone(9)
    send(6, sel_o, x_o.at[:, lanes(1, H)], (cross, sp), cross_ok, cross_ok)
    send(7, sel_o.at[:, lanes(H - 1, 1)], x_o.at[:, lanes(0, 1)], (cross, sp + 1), cross_ok & up_ok, cross_ok & dn_ok)
    send(8, sel_o.at[:, lanes(0, 1)], x_o.at[:, lanes(H + 1, 1)], (cross, sp - 1), cross_ok & dn_ok, cross_ok & up_ok)

    arrive(4)
    arrive(5)
    for c in (ODD, EVEN):
        put(stack, lanes(0, H + 2), pick(c, tcur[0], tcur[1]))
        p1_cur[c] = conv(w_fwd[c, 0], stack[:, lanes(0, H + 2)])
    for c, halo in ((EVEN, 2), (ODD, 5)):
        arrive(12 + 8 * c, 13 + 8 * c)
        rows = H + 2 * halo
        put(stack_g, lanes(0, rows), ccot[c, :, lanes(5 - halo, rows)].astype(F32), flip=True)
        g4[c][...] = conv(w_bwd[c, 3], stack_g[:, lanes(0, rows)], flip=True)

    arrive(2)
    arrive(3)
    first_core = core == 0
    reach = (7, 4)

    def layer_one(c, outer, inner):
        put(stack_c, lanes(0, H + 2), jnp.where(first_core, outer, inner))
        put(stack_c, lanes(0, H + 2), jnp.where(first_core, inner, outer), base=3 * C)
        pre = p1_cur[c] + conv(w_ctx[c], stack_c[...])
        halo = reach[c]
        p1[c][:, lanes(halo, H)] = pre
        h1_s[c][0] = pre[:, lanes(H - halo, halo)].astype(BF)
        h1_s[c][1] = pre[:, lanes(0, halo)].astype(BF)
        send(14 + 2 * c, h1_s[c].at[0], h1_r[c].at[0], (tm, sp + 1), up_ok, dn_ok)
        send(15 + 2 * c, h1_s[c].at[1], h1_r[c].at[1], (tm, sp - 1), dn_ok, up_ok)

    def activate(pre, halo):
        sigma = 1.0 / (1.0 + jnp.exp(-pre))
        act = pre * sigma
        slope = sigma * (1.0 + pre * (1.0 - sigma))
        row = (lax.broadcasted_iota(jnp.int32, pre.shape, 1) >> 7) + (sp * H - halo)
        inside = (row >= 0) & (row < ns * H)
        return jnp.where(inside, act, 0.0), jnp.where(inside, slope, 0.0)

    def forward(c):
        h = reach[c]
        arrive(14 + 2 * c, 15 + 2 * c)
        p1[c][:, lanes(0, h)] = h1_r[c][0].astype(F32)
        p1[c][:, lanes(H + h, h)] = h1_r[c][1].astype(F32)
        act, slope = activate(p1[c][...], h)
        d1[c] = slope[:, lanes(h - 1, H + 2)]
        for k in (1, 2, 3):
            rows = lanes(0, H + 2 * (h + 1 - k))
            put(stack, rows, act)
            act, slope = activate(conv(w_fwd[c, k], stack[:, rows]), h - k)
            if k == 1:
                d2[c] = slope[:, lanes(h - 3, H + 4)]
            if k == 2:
                d3[c][...] = slope[:, lanes(2, H + 2 * (h - 4))]
        rows = lanes(0, H + 2 * (h - 3))
        put(stack_g, rows, g4[c][...] * slope, flip=True)
        s3 = conv(w_bwd[c, 2], stack_g[:, rows], flip=True) * d3[c][...]
        if c == EVEN:
            h3_s[0] = s3[:, lanes(H - 3, 3)].astype(BF)
            h3_s[1] = s3[:, lanes(0, 3)].astype(BF)
            send(18, h3_s.at[0], h3_r.at[0], (tm, sp + 1), up_ok, dn_ok)
            send(19, h3_s.at[1], h3_r.at[1], (tm, sp - 1), dn_ok, up_ok)
        put(stack_3.at[c], lanes(7 - h, H + 2 * (h - 4)), s3, flip=True)
        put(stack_4.at[c], lanes(0, H + 2), act[:, lanes(h - 4, H + 2)])

    def finish(c):
        own = pick(c, tcur[0, :, lanes(1, H)], tcur[1, :, lanes(1, H)])
        outs[c] = own + conv(w_fwd[c, 4], stack_4[c])

    def backward(c):
        if c == EVEN:
            arrive(18, 19)
            put(stack_3.at[c], lanes(0, 3), h3_r[0].astype(F32), flip=True)
            put(stack_3.at[c], lanes(H + 3, 3), h3_r[1].astype(F32), flip=True)
        s2 = conv(w_bwd[c, 1], stack_3[c], flip=True) * d2[c]
        put(stack_g, lanes(0, 20), s2, flip=True)
        s1 = conv(w_bwd[c, 0], stack_g[:, lanes(0, 20)], flip=True) * d1[c]
        put(stack_g, lanes(0, 18), s1, flip=True)
        grads = conv(w_back[c], stack_g[:, lanes(0, 18)], flip=True, out_channels=2 * C)
        behind, ahead = grads[:C], grads[C:]
        return jnp.where(first_core, behind, ahead), jnp.where(first_core, ahead, behind)

    arrive(9, 10, 11)
    send(22, x_l, m_l, (mate, sp), cross_ok, mate_cross_ok)
    arrive(22)
    inner = jnp.where(has_l, m_l[...].astype(F32), pick(EVEN, mctx[0], mctx[1]))
    layer_one(EVEN, x_l[...].astype(F32), inner)
    arrive(6, 7, 8)
    layer_one(ODD, x_o[...].astype(F32), pick(ODD, mctx[0], mctx[1]))
    forward(EVEN)
    outer_g, inner_g = backward(EVEN)
    em_s[...] = inner_g.astype(BF)
    send(25, em_s, em_r, (mate, sp), always, always)
    finish(EVEN)
    arrive(25)
    from_mate = em_r[...].astype(F32)
    ex_s[...] = (outer_g + jnp.where(has_l, 0.0, from_mate)).astype(BF)
    send(26, ex_s, ex_r, (cross, sp), cross_ok, cross_ok)
    forward(ODD)
    outer_g, inner_g = backward(ODD)
    ox_s[...] = outer_g.astype(BF)
    send(23, ox_s, ox_r, (cross, sp), cross_ok, cross_ok)
    om_s[...] = inner_g.astype(BF)
    send(24, om_s, om_r, (mate, sp), always, always)
    finish(ODD)
    mask = wide(H)

    def channels_first(dst, i, value):
        for r in range(H):
            flat[pl.ds(r, C, stride=H), :] = value[:, lanes(r, 1)]
        dst[i] = flat[...].reshape(C, H, W).astype(dst.dtype)

    channels_first(out, 0, jnp.where(mask, outs[EVEN], outs[ODD]))
    channels_first(out, 1, jnp.where(mask, outs[ODD], outs[EVEN]))
    arrive(26)
    send(27, ex_r, ey_r, (mate, sp), cross_ok, mate_cross_ok)
    arrive(27)
    even_g = ex_r[...].astype(F32) + ey_r[...].astype(F32) + em_r[...].astype(F32)
    even_g = jnp.where(has_l, even_g, 0.0)
    arrive(24, 23)
    odd_g = ox_r[...].astype(F32) + om_r[...].astype(F32)
    channels_first(rg, 0, jnp.where(mask, even_g, odd_g))
    channels_first(rg, 1, jnp.where(mask, odd_g, even_g))
    gone(*(i for i in sent if i not in left))


def solution(mesh):
    nt, ns = mesh.shape["tm"], mesh.shape["space"]

    def on_device(current, contexts, cotangent, level_table, ref_table, w_first, w_rest):
        vmem = pl.BlockSpec(memory_space=pltpu.VMEM)

        def bf(*shape):
            return pltpu.VMEM(shape, BF)

        def f32(*shape):
            return pltpu.VMEM(shape, F32)

        slab = H * W
        halo = (H + 2) * W
        scratch = [
            bf(2, C, H, W), bf(2, C, H, W), bf(2, C, H, W), bf(2, 9, C, 3 * C), bf(2, 4, 9, C, C),
            f32(C * H, W), bf(2, C, slab), bf(16, W), bf(16, W), bf(2, C, halo), bf(C, slab), bf(C, slab),
            bf(C, halo), bf(C, halo), bf(C, halo), bf(2, C, halo), bf(2, C, slab), bf(2, C, (H + 10) * W),
            bf(3 * C, 30 * W), bf(6 * C, halo), bf(3 * C, 26 * W), bf(2, 3 * C, 22 * W), bf(2, 3 * C, halo),
            f32(2, C, slab), f32(C, 24 * W), f32(C, halo), f32(C, 30 * W), f32(C, 24 * W),
            f32(2, C, halo), f32(2, C, (H + 4) * W), f32(C, 22 * W), f32(C, slab), f32(2, C, slab),
            bf(2, C, 7 * W), bf(2, C, 7 * W), bf(2, C, 4 * W), bf(2, C, 4 * W), bf(2, C, 3 * W), bf(2, C, 3 * W),
            bf(C, slab), bf(C, slab), bf(C, slab), bf(C, slab),
            bf(C, slab), bf(C, slab), bf(C, slab), bf(C, slab), bf(C, slab),
            bf(2, 5, 3 * C, 3 * C), bf(2, 4, 3 * C, 3 * C), bf(2, 3 * C, 6 * C), bf(2, 6 * C, 3 * C),
            pltpu.SemaphoreType.DMA((29,)), pltpu.SemaphoreType.DMA((29,)), pltpu.SemaphoreType.DMA((5,)),
        ]

        def kernel(*refs):
            body(nt, ns, *refs)

        out, rg = pl.pallas_call(
            kernel,
            out_shape=(
                jax.ShapeDtypeStruct((2, C, H, W), F32),
                jax.ShapeDtypeStruct((2, C, H, W), F32),
            ),
            in_specs=[pl.BlockSpec(memory_space=pltpu.SMEM)] + [pl.BlockSpec(memory_space=pl.ANY)] * 5,
            out_specs=(vmem, vmem),
            scratch_shapes=scratch,
            compiler_params=pltpu.CompilerParams(
                collective_id=0, has_side_effects=True, vmem_limit_bytes=56 << 20
            ),
            name="coding",
        )(level_table, current, contexts, cotangent, w_first, w_rest)
        return out.astype(BF), rg

    frames = P("tm", None, "space", None)
    return jax.shard_map(
        on_device,
        mesh=mesh,
        in_specs=(frames, frames, frames, P("tm"), P("tm", None), P(), P()),
        out_specs=(frames, frames),
        check_vma=False,
    )
```
